32 devices in a mesh: grp: 2 (over x), node: 16 (over z, y, core).
Axes of the slice: x: 2, y: 2, z: 4, core: 2. Of those that a mesh axis runs over, the one named last changes fastest.
Arguments:
- queries: bfloat16 [32, 4, 16384], P(('grp', 'node')), parts along dimension 0, may hold values from -150 to 150
- shared_kv: bfloat16 [2, 24576, 1024], P(None, ('grp', 'node')), parts along dimension 1, may hold values from -12 to 12
- page_mask: int32 [192, 16], P(('grp', 'node')), parts along dimension 0, may hold values from 0 to 1, as said below
- slot_request: int32 [32], P('grp'), parts along dimension 0, may hold values from 0 to 15, each once
- suffix_blocks: int32 [32], P(('grp', 'node')), parts along dimension 0, may hold values from 1 to 2, as said below
- suffix_kv: bfloat16 [32, 2, 256, 1024], P(('grp', 'node')), parts along dimension 0, may hold values from -8 to 8
- new_kv: bfloat16 [32, 2, 4, 1024], P(('grp', 'node')), parts along dimension 0, may hold values from -12 to 12
Outputs:
- attn_out: bfloat16 [32, 4, 16384], P(('grp', 'node')), parts along dimension 0
The draws below stay inside these ranges and needn't reach their ends.
There are 2 independent parts, one for each index of `grp`. The reference program is written for one: setup_inputs(seed, part) draws one part's arguments, and reference() takes and returns one part's arrays. A program takes and returns all parts, laid end to end along the dimension named above; each array names one. Nothing has to cross between parts.
Inputs may be any that keep to these rules, and one draw needn't show every extreme that they name: page_mask[p, r] is 1 for the 32 pages of the system prompt and for the 32 pages of the prefix of request r's group (2 groups, each request in one), else 0. `suffix_blocks`: some slot has exactly 2.
All inputs are finite; a program needn't handle non-finite values.
Results may differ from the reference program's by a relative error of at most 0.008.
Values may be sent and summed in bfloat16 or wider, within the bound.
A program may use at most 128 MiB of HBM per device.

```python
import jax
import jax.numpy as jnp
from jax import lax

H = 128
KVH = 8
DH = 128
STEPS = 4
BT = 128
GPB = 32
SUF_MAX = 2
BLK_DEV = 6
PAGES = 96
GROUPS = 2
SYS_PAGES = 32
REQUESTS = 16


def tree_layout(key):
    page_kinds = jnp.concatenate([jnp.full((SYS_PAGES,), -1, jnp.int32), jnp.repeat(jnp.arange(GROUPS, dtype=jnp.int32), GPB, total_repeat_length=GROUPS * GPB)])
    page_order = jax.random.permutation(jax.random.fold_in(key, 11), PAGES)
    page_group = page_kinds[page_order]
    draw_one = jax.random.randint(jax.random.fold_in(key, 12), (REQUESTS,), 0, GROUPS)
    draw_two = jax.random.randint(jax.random.fold_in(key, 13), (REQUESTS,), 0, GROUPS)
    skewed = jnp.minimum(draw_one, draw_two)
    request_ids = jnp.arange(REQUESTS, dtype=jnp.int32)
    grouped = jnp.where(request_ids < GROUPS, request_ids % GROUPS, skewed)
    labels = jax.random.permutation(jax.random.fold_in(key, 14), GROUPS)
    grouped = labels[grouped]
    shuffle = jax.random.permutation(jax.random.fold_in(key, 15), REQUESTS)
    return (page_group, grouped[shuffle])


def shared_keys(key):
    drawn = jnp.clip(1.5 * jax.random.normal(jax.random.fold_in(key, 21), (PAGES * BT, KVH * DH), jnp.float32), -9.0, 9.0)
    paired = drawn.reshape(PAGES * BT // 2, 2, KVH * DH)
    second = paired[:, 1]
    return jnp.stack([paired[:, 0], second], axis=1).reshape(PAGES * BT, KVH * DH)


def query_base(key):
    return jax.random.normal(jax.random.fold_in(key, 31), (REQUESTS, STEPS, H * DH), jnp.float32)


def draw_page_mask(key, part):
    page_group, request_group = tree_layout(key)
    visible = (page_group[:, None] < 0) | (page_group[:, None] == request_group[None, :])
    return visible.astype(jnp.int32)


def draw_shared_kv(key, part):
    key_rows = shared_keys(key)
    key = jax.random.fold_in(key, 2)
    value_rows = 1.5 * jax.random.normal(key, (PAGES * BT, KVH * DH), jnp.float32)
    value_rows = jnp.clip(value_rows, -12.0, 12.0)
    return jnp.stack([key_rows, value_rows], axis=0).astype(jnp.bfloat16)


def draw_queries(key, part):
    base = query_base(key)
    queries = jnp.clip(1.67 * base, -10.0, 10.0)
    return queries.astype(jnp.bfloat16)


def draw_new_kv(key, part):
    base = query_base(key)
    key = jax.random.fold_in(key, 4)
    grouped = jnp.mean(base.reshape(REQUESTS, STEPS, KVH, H // KVH, DH), axis=3).reshape(REQUESTS, STEPS, KVH * DH)
    recent_keys = 8.3 * grouped + 0.5 * jax.random.normal(jax.random.fold_in(key, 61), (REQUESTS, STEPS, KVH * DH), jnp.float32)
    recent_values = 1.5 * jax.random.normal(jax.random.fold_in(key, 62), (REQUESTS, STEPS, KVH * DH), jnp.float32)
    return jnp.clip(jnp.stack([recent_keys, recent_values], axis=1), -12.0, 12.0).astype(jnp.bfloat16)


def draw_suffix_blocks(key, part):
    key = jax.random.fold_in(key, 5)
    lengths = jax.random.randint(jax.random.fold_in(key, 71), (REQUESTS,), 1, SUF_MAX + 1)
    longest = jax.random.randint(jax.random.fold_in(key, 72), (), 0, REQUESTS)
    return lengths.at[longest].set(SUF_MAX).astype(jnp.int32)


def steps_of(rng, dims, split, least, largest):
    def one(dim, blocks):
        steps = jax.random.uniform(jax.random.fold_in(jax.random.fold_in(rng, 6), dim), (blocks,), jnp.float32, least / len(split), largest / len(split))
        return jnp.repeat(jnp.exp(steps), dims[dim] // blocks).reshape((-1,) + (1,) * (len(dims) - dim - 1))

    factor_of = one(*split[0])
    for cut in split[1:]:
        factor_of = factor_of * one(*cut)
    return factor_of


def centred(own_key, dims, width, reach, shards=(), kind=jnp.bfloat16):
    values = width * jax.random.normal(own_key, dims, jnp.float32)
    if shards:
        values = values * steps_of(own_key, dims, shards, -0.22, 0.18)
    return jnp.clip(values, -reach, reach).astype(kind)


def setup_inputs(seed: int = 0, part: int = 0) -> dict:
    seeds = jax.random.split(jax.random.key(seed), 8)
    own_keys = jax.random.split(jax.random.fold_in(seeds[7], part), 8)
    return {
        "queries": draw_queries(jax.random.fold_in(jax.random.fold_in(seeds[7], part), 71), part),
        "shared_kv": draw_shared_kv(jax.random.fold_in(jax.random.fold_in(seeds[7], part), 71), part),
        "page_mask": draw_page_mask(jax.random.fold_in(jax.random.fold_in(seeds[7], part), 71), part),
        "slot_request": jax.random.permutation(own_keys[3], REQUESTS).astype(jnp.int32),
        "suffix_blocks": draw_suffix_blocks(jax.random.fold_in(jax.random.fold_in(seeds[7], part), 71), part),
        "suffix_kv": centred(own_keys[5], (REQUESTS, 2, SUF_MAX * BT, KVH * DH), 1.5, 8.0, ((0, 16),)),
        "new_kv": draw_new_kv(jax.random.fold_in(jax.random.fold_in(seeds[7], part), 71), part),
    }


MASKED_SCORE = -1e30


def rounded(values):
    return lax.optimization_barrier(values.astype(jnp.bfloat16)).astype(jnp.float32)


def reference(queries, shared_kv, page_mask, slot_request, suffix_blocks, suffix_kv, new_kv):
    group_size = H // KVH
    scaling = DH ** -0.5
    set_count = PAGES // BLK_DEV
    key_rows = shared_kv[0].astype(jnp.float32).reshape(set_count, BLK_DEV * BT, KVH, DH)
    value_rows = shared_kv[1].astype(jnp.float32).reshape(set_count, BLK_DEV * BT, KVH, DH)
    selector = (jnp.arange(REQUESTS)[:, None] == slot_request[None, :]).astype(jnp.int32)
    visible = jnp.dot(page_mask, selector)
    slot_pages = visible.T.reshape(REQUESTS, set_count, BLK_DEV)

    def one_slot(slot_items):
        query, pages, suffix_pairs, live_count, new_pairs = slot_items
        query_heads = query.astype(jnp.float32).reshape(STEPS, KVH, group_size, DH)
        scores = jnp.einsum("skgd,ntkd->nskgt", query_heads, key_rows) * scaling
        allowed = (jnp.repeat(pages, BT, axis=1) > 0)[:, None, None, None, :]
        scores = jnp.where(allowed, scores, MASKED_SCORE)
        set_max = jnp.max(scores, axis=-1)
        weights = jnp.where(allowed, jnp.exp(scores - set_max[..., None]), 0.0)
        totals = jnp.sum(weights, axis=-1)
        outputs = jnp.einsum("nskgt,ntkd->nskgd", rounded(weights), value_rows)
        parts = rounded(outputs / jnp.maximum(totals, 1.0)[..., None])
        cached_keys = suffix_pairs[0].astype(jnp.float32).reshape(SUF_MAX * BT, KVH, DH)
        cached_values = suffix_pairs[1].astype(jnp.float32).reshape(SUF_MAX * BT, KVH, DH)
        recent_keys = new_pairs[0].astype(jnp.float32).reshape(STEPS, KVH, DH)
        recent_values = new_pairs[1].astype(jnp.float32).reshape(STEPS, KVH, DH)
        cached = jnp.einsum("skgd,tkd->skgt", query_heads, cached_keys) * scaling
        recent = jnp.einsum("skgd,jkd->skgj", query_heads, recent_keys) * scaling
        cached_allowed = ((jnp.arange(SUF_MAX * BT) // BT) < live_count)[None, None, None, :]
        causal = jnp.arange(STEPS)[None, :] <= jnp.arange(STEPS)[:, None]
        recent_allowed = causal[:, None, None, :]
        cached = jnp.where(cached_allowed, cached, MASKED_SCORE)
        recent = jnp.where(recent_allowed, recent, MASKED_SCORE)
        own_max = jnp.maximum(jnp.max(cached, axis=-1), jnp.max(recent, axis=-1))
        cached_weights = jnp.where(cached_allowed, jnp.exp(cached - own_max[..., None]), 0.0)
        recent_weights = jnp.where(recent_allowed, jnp.exp(recent - own_max[..., None]), 0.0)
        own_totals = jnp.sum(cached_weights, axis=-1) + jnp.sum(recent_weights, axis=-1)
        own_outputs = jnp.einsum("skgt,tkd->skgd", rounded(cached_weights), cached_values)
        own_outputs = own_outputs + jnp.einsum("skgj,jkd->skgd", rounded(recent_weights), recent_values)
        own_parts = rounded(own_outputs / jnp.maximum(own_totals, 1.0)[..., None])
        row_max = jnp.maximum(jnp.max(set_max, axis=0), own_max)
        factor = jnp.exp(set_max - row_max) * totals
        own_factor = jnp.exp(own_max - row_max) * own_totals
        numerator = jnp.sum(factor[..., None] * parts, axis=0) + own_factor[..., None] * own_parts
        denominator = jnp.sum(factor, axis=0) + own_factor
        return (numerator / denominator[..., None]).reshape(STEPS, H * DH).astype(jnp.bfloat16)

    return lax.map(one_slot, (queries, slot_pages, suffix_kv, suffix_blocks, new_kv))
```

```python
import functools

import jax
import jax.numpy as jnp
import numpy as np
from jax import lax
from jax.experimental import pallas as pl
from jax.experimental.pallas import tpu as pltpu
from jax.sharding import PartitionSpec as P

H = 128
KVH = 8
DH = 128
BT = 128
STEPS = 4
G = H // KVH
HALF = KVH // 2
ROWS = STEPS * G
LANES = 2 * ROWS
SCALE2 = float(DH ** (-0.5) * np.log2(np.e))
BIG = 1e30
F32 = jnp.float32
BF16 = jnp.bfloat16
NT = (((1,), (1,)), ((), ()))


def merge(o1, l1, o2, l2):
    top = jnp.maximum(l1, l2)
    a, b = jnp.exp2(l1 - top), jnp.exp2(l2 - top)
    both = a + b
    inv = 1.0 / both
    return o1 * (a * inv) + o2 * (b * inv), top + jnp.log2(both)


def attend(q, segments):
    scores, top = [], None
    for keys, _, penalty in segments:
        s = lax.dot_general(keys, q, NT, preferred_element_type=F32)
        scores.append(s)
        if penalty.shape[0] == 1:
            m = jnp.max(s, axis=0, keepdims=True) - penalty
        else:
            m = jnp.max(s - penalty, axis=0, keepdims=True)
        top = m if top is None else jnp.maximum(top, m)
    out, total = None, None
    for s, (_, values, penalty) in zip(scores, segments):
        w = jnp.exp2((s - jnp.where(penalty > 0, BIG, top)) * SCALE2)
        t = jnp.sum(w, axis=0, keepdims=True)
        o = jnp.dot(values, w.astype(BF16), preferred_element_type=F32)
        total = t if total is None else total + t
        out = o if out is None else out + o
    live = total > 0
    inv = 1.0 / jnp.where(live, total, 1.0)
    lse = jnp.where(live, top * SCALE2 + jnp.log2(jnp.where(live, total, 1.0)), -BIG)
    return out * inv, lse


def kernel(
    chips, tokens, q_ref, kv_ref, suf_ref, new_ref, bias_ref, out_ref,
    qb, kvs, sufs, news, bias, vt, svt, part_o, part_l, rs_in, rs_out, rl_in, rl_out, fin, land,
    loc_sem, sib_send, sib_recv, g_send, g_recv, o_send, o_recv, l_send, l_recv, f_send, f_recv,
):
    half = chips // 2
    node = lax.axis_index("node")
    core, chip = lax.rem(node, 2), lax.div(node, 2)
    odd, pair_no = lax.rem(chip, 2), lax.div(chip, 2)
    pos = (1 - odd) * pair_no + odd * (chips - 1 - pair_no)

    def at(position):
        back = lax.div(position, half)
        place = (1 - back) * 2 * position + back * (2 * (chips - 1 - position) + 1)
        return {"node": place * 2 + core}

    sibling = {"node": node + 1 - 2 * core}
    ahead = (at(lax.rem(pos + 1, chips)), at(lax.rem(pos + chips - 1, chips)))
    pages = tokens // BT

    def behind(d, k):
        return lax.rem(pos + chips - k, chips) if d == 0 else lax.rem(pos + k, chips)

    mine = pl.multiple_of(core * HALF * DH, HALF * DH)
    theirs = pl.multiple_of((1 - core) * HALF * DH, HALF * DH)
    slot_rows = pl.ds(pl.multiple_of(core * ROWS, ROWS), ROWS)

    def views(columns, heads):
        return (
            (q_ref.at[pl.ds(heads, HALF)], qb.at[pos, :, slot_rows, :]),
            (bias_ref, bias.at[core]),
            (kv_ref.at[:, :, pl.ds(columns, HALF * DH)], kvs.at[:, core]),
            (suf_ref.at[:, :, pl.ds(columns, HALF * DH)], sufs.at[:, core]),
            (new_ref.at[:, :, pl.ds(columns, HALF * DH)], news.at[:, core]),
        )

    local = [
        pltpu.make_async_copy(src, dst, loc_sem.at[i])
        for i, (src, dst) in enumerate(views(mine, core * HALF))
    ]
    across = [
        pltpu.make_async_remote_copy(
            src_ref=src, dst_ref=dst, send_sem=sib_send.at[i], recv_sem=sib_recv.at[i],
            device_id=sibling,
        )
        for i, (src, dst) in enumerate(views(theirs, (1 - core) * HALF))
    ]

    def hop(d, h, piece):
        ref = qb.at[behind(d, h - 1), pl.ds(2 * piece, 2)]
        return pltpu.make_async_remote_copy(
            src_ref=ref, dst_ref=ref, send_sem=g_send.at[d, h, piece],
            recv_sem=g_recv.at[d, h, piece], device_id=ahead[d],
        )

    def landed(d, h, piece):
        ref = qb.at[behind(d, h), pl.ds(2 * piece, 2)]
        return pltpu.make_async_remote_copy(
            src_ref=ref, dst_ref=ref, send_sem=g_send.at[d, h, piece],
            recv_sem=g_recv.at[d, h, piece], device_id=ahead[d],
        )

    def stage(d, j, piece):
        heads = pl.ds(2 * piece, 2)
        return (
            pltpu.make_async_remote_copy(
                src_ref=rs_out.at[d, j, heads], dst_ref=rs_in.at[d, j, heads],
                send_sem=o_send.at[d, j, piece], recv_sem=o_recv.at[d, j, piece],
                device_id=ahead[d],
            ),
            pltpu.make_async_remote_copy(
                src_ref=rl_out.at[d, j, piece], dst_ref=rl_in.at[d, j, piece],
                send_sem=l_send.at[d, j, piece], recv_sem=l_recv.at[d, j, piece],
                device_id=ahead[d],
            ),
        )

    for copy in local:
        copy.start()
    barrier = pltpu.get_barrier_semaphore()
    for other in (sibling, *ahead):
        pl.semaphore_signal(barrier, inc=1, device_id=other)
    pl.semaphore_wait(barrier, 3)
    for copy in across:
        copy.start()
    local[0].wait()
    across[0].wait_recv()
    for piece in range(2):
        for d in range(2):
            hop(d, 1, piece).start()
    for copy in local[1:]:
        copy.wait()
    for copy in across[1:]:
        copy.wait_recv()

    def columns_of(k):
        return pl.ds(pl.multiple_of(k * DH, DH), DH)

    @pl.loop(0, HALF)
    def _(k):
        for s in range(2):
            vt[k, s] = kvs[1, s, :, columns_of(k)].T
            svt[k, s] = sufs[1, s, :, columns_of(k)].T

    def shared_segments(k, blocks):
        found = []
        for s in range(2):
            for page in range(pages):
                rows = slice(page * BT, (page + 1) * BT)
                penalty = jnp.concatenate([bias[s, b, page : page + 1, :] for b in blocks], axis=1)
                found.append((kvs[0, s, rows, columns_of(k)], vt[k, s, :, rows], penalty))
        return found

    def keep(block, k, o, lse):
        part_o[block, k] = o
        part_l[block, k] = lse

    def own_block():
        token = lax.broadcasted_iota(jnp.int32, (16, LANES), 0)
        lane = lax.broadcasted_iota(jnp.int32, (16, LANES), 1)
        step = lax.rem(lax.div(lane, G), STEPS)

        @pl.loop(0, HALF)
        def _(k):
            found = shared_segments(k, [pos])
            for s in range(2):
                for page in range(sufs.shape[2] // BT):
                    rows = slice(page * BT, (page + 1) * BT)
                    penalty = bias[s, chips, page : page + 1, :]
                    found.append((sufs[0, s, rows, columns_of(k)], svt[k, s, :, rows], penalty))
                seen = (token <= step) & (lax.div(lane, ROWS) == s)
                found.append(
                    (
                        news[0, s, :, columns_of(k)],
                        news[1, s, :, columns_of(k)].T,
                        jnp.where(seen, 0.0, BIG),
                    )
                )
            keep(pos, k, *attend(qb[pos, k], found))

    def one_block(block):
        @pl.loop(0, HALF)
        def _(k):
            keep(block, k, *attend(qb[block, k], shared_segments(k, [block])))

    def two_blocks(a, b):
        @pl.loop(0, HALF)
        def _(k):
            q = jnp.concatenate([qb[a, k], qb[b, k]], axis=0)
            o, lse = attend(q, shared_segments(k, [a, b]))
            keep(a, k, o[:, :LANES], lse[:, :LANES])
            keep(b, k, o[:, LANES:], lse[:, LANES:])

    def pass_on(h):
        for piece in range(2):
            for d in range(2):
                landed(d, h, piece).wait_recv()

                @pl.when((h + 1 < half) | (d == piece))
                def _():
                    hop(d, h + 1, piece).start()

    pass_on(1)
    own_block()

    @pl.loop(2, half + 1)
    def _(h):
        @pl.when(h < half)
        def _():
            pass_on(h)

        @pl.when(h == half)
        def _():
            for d in range(2):
                landed(d, half, d).wait_recv()
            far = behind(0, half)
            one_block(far)
            for d in range(2):
                for i in range(2):
                    k = 2 * d + i
                    rs_out[d, 1, k] = part_o[far, k].astype(BF16)
                    rl_out[d, 1, d, i : i + 1, :] = part_l[far, k]
                for copy in stage(d, 1, d):
                    copy.start()

        two_blocks(behind(0, h - 1), behind(1, h - 1))

    def incoming(d, j, piece):
        for copy in stage(d, j, piece):
            copy.wait_recv()

    def received(d, j, k):
        return rs_in[d, j, k].astype(F32), rl_in[d, j, k // 2, k % 2 : k % 2 + 1, :]

    @pl.loop(2, half + 1)
    def _(j):
        for piece in range(2):
            for d in range(2):
                target = behind(1 - d, half + 1 - j)

                def add():
                    incoming(d, j - 1, piece)
                    for k in (2 * piece, 2 * piece + 1):
                        o, lse = merge(*received(d, j - 1, k), part_o[target, k], part_l[target, k])
                        rs_out[d, j, k] = o.astype(BF16)
                        rl_out[d, j, piece, k % 2 : k % 2 + 1, :] = lse

                def begin():
                    for k in (2 * piece, 2 * piece + 1):
                        rs_out[d, j, k] = part_o[target, k].astype(BF16)
                        rl_out[d, j, piece, k % 2 : k % 2 + 1, :] = part_l[target, k]

                if d == piece:
                    add()
                else:
                    pl.when(j > 2)(add)
                    pl.when(j == 2)(begin)
                for copy in stage(d, j, piece):
                    copy.start()

    for piece in range(2):
        for d in range(2):
            incoming(d, half, piece)
        for k in (2 * piece, 2 * piece + 1):
            o, lse = merge(*received(0, half, k), part_o[pos, k], part_l[pos, k])
            o, _ = merge(o, lse, *received(1, half, k))
            fin[k] = o.T.astype(BF16)
    sib_rows = pl.ds(pl.multiple_of((1 - core) * ROWS, ROWS), ROWS)
    give = pltpu.make_async_remote_copy(
        src_ref=fin.at[:, sib_rows, :], dst_ref=land, send_sem=f_send, recv_sem=f_recv,
        device_id=sibling,
    )
    give.start()
    out_ref[pl.ds(core * HALF, HALF)] = fin[:, slot_rows, :]
    give.wait_recv()
    out_ref[pl.ds((1 - core) * HALF, HALF)] = land[...]
    give.wait_send()
    for copy in across:
        copy.wait_send()

    @pl.loop(1, half + 1)
    def _(h):
        for piece in range(2):
            for d in range(2):
                @pl.when((h < half) | (d == piece))
                def _():
                    hop(d, h, piece).wait_send()

                @pl.when((h > 1) | (d == piece))
                def _():
                    for copy in stage(d, h, piece):
                        copy.wait_send()


def ring_order(chips):
    return np.array([2 * r if r < chips // 2 else 2 * (chips - 1 - r) + 1 for r in range(chips)])


def per_device(queries, shared_kv, page_mask, slot_request, suffix_blocks, suffix_kv, new_kv):
    nodes = lax.axis_size("node")
    chips = nodes // 2
    half = chips // 2
    tokens = shared_kv.shape[1]
    suffix_tokens = suffix_kv.shape[2]
    core = lax.rem(lax.axis_index("node"), 2)

    q = queries.reshape(STEPS, KVH, G, DH).transpose(1, 0, 2, 3).reshape(KVH, ROWS, DH)
    new = jnp.pad(new_kv[0], ((0, 0), (0, 16 - STEPS), (0, 0)))
    selector = (slot_request[:, None] == jnp.arange(page_mask.shape[1])[None, :])
    visible = jnp.sum(
        jnp.where(selector[None], page_mask[:, None, :], 0), axis=-1
    )
    blocks = visible.reshape(-1, chips, 2)[:, ring_order(chips), :].transpose(1, 0, 2)
    suffix_live = (jnp.arange(blocks.shape[1]) < suffix_blocks[0])[:, None] & (
        jnp.arange(2) == core
    )[None, :]
    allowed = jnp.concatenate([blocks > 0, suffix_live[None]], axis=0)
    bias = jnp.where(allowed, 0.0, BIG).astype(F32)
    bias = jnp.repeat(bias, ROWS, axis=-1)
    bias = jnp.pad(bias, ((0, 0), (0, -bias.shape[1] % 8), (0, 0)))

    dma = pltpu.SemaphoreType.DMA
    grid_sems = dma((2, half + 1, 2))
    out = pl.pallas_call(
        functools.partial(kernel, chips, tokens),
        out_shape=jax.ShapeDtypeStruct((KVH, ROWS, DH), BF16),
        in_specs=[pl.BlockSpec(memory_space=pl.ANY)] * 5,
        out_specs=pl.BlockSpec(memory_space=pltpu.VMEM),
        scratch_shapes=[
            pltpu.VMEM((chips, HALF, LANES, DH), BF16),
            pltpu.VMEM((2, 2, tokens, HALF * DH), BF16),
            pltpu.VMEM((2, 2, suffix_tokens, HALF * DH), BF16),
            pltpu.VMEM((2, 2, 16, HALF * DH), BF16),
            pltpu.VMEM((2,) + bias.shape, F32),
            pltpu.VMEM((HALF, 2, DH, tokens), BF16),
            pltpu.VMEM((HALF, 2, DH, suffix_tokens), BF16),
            pltpu.VMEM((chips, HALF, DH, LANES), F32),
            pltpu.VMEM((chips, HALF, 1, LANES), F32),
            pltpu.VMEM((2, half + 1, HALF, DH, LANES), BF16),
            pltpu.VMEM((2, half + 1, HALF, DH, LANES), BF16),
            pltpu.VMEM((2, half + 1, 2, 8, LANES), F32),
            pltpu.VMEM((2, half + 1, 2, 8, LANES), F32),
            pltpu.VMEM((HALF, LANES, DH), BF16),
            pltpu.VMEM((HALF, ROWS, DH), BF16),
            dma((5,)), dma((5,)), dma((5,)),
            grid_sems, grid_sems, grid_sems, grid_sems, grid_sems, grid_sems,
            dma, dma,
        ],
        compiler_params=pltpu.CompilerParams(
            collective_id=0, has_side_effects=True, vmem_limit_bytes=56 * 1024 * 1024
        ),
    )(q, shared_kv, suffix_kv[0], new, bias)
    out = out.reshape(KVH, STEPS, G, DH).transpose(1, 0, 2, 3)
    return out.reshape(1, STEPS, H * DH)


def solution(mesh):
    placed = (
        P(("grp", "node"), None, None),
        P(None, ("grp", "node"), None),
        P(("grp", "node"), None),
        P("grp"),
        P(("grp", "node")),
        P(("grp", "node"), None, None, None),
        P(("grp", "node"), None, None, None),
    )
    return jax.shard_map(
        per_device,
        mesh=mesh,
        in_specs=placed,
        out_specs=P(("grp", "node"), None, None),
        check_vma=False,
    )
```

```python
import functools

import jax
import jax.numpy as jnp
import numpy as np
from jax import lax
from jax.experimental import pallas as pl
from jax.experimental.pallas import tpu as pltpu
from jax.sharding import PartitionSpec as P

H = 128
KVH = 8
DH = 128
BT = 128
STEPS = 4
G = H // KVH
HALF = KVH // 2
ROWS = STEPS * G
LANES = 2 * ROWS
SCALE2 = float(DH ** (-0.5) * np.log2(np.e))
BIG = 1e30
F32 = jnp.float32
BF16 = jnp.bfloat16
NT = (((1,), (1,)), ((), ()))


def merge(o1, l1, o2, l2):
    top = jnp.maximum(l1, l2)
    a, b = jnp.exp2(l1 - top), jnp.exp2(l2 - top)
    both = a + b
    inv = 1.0 / both
    return o1 * (a * inv) + o2 * (b * inv), top + jnp.log2(both)


def attend(q, segments):
    scores, top = [], None
    for keys, _, penalty in segments:
        s = lax.dot_general(keys, q, NT, preferred_element_type=F32)
        scores.append(s)
        if penalty.shape[0] == 1:
            m = jnp.max(s, axis=0, keepdims=True) - penalty
        else:
            m = jnp.max(s - penalty, axis=0, keepdims=True)
        top = m if top is None else jnp.maximum(top, m)
    out, total = None, None
    for s, (_, values, penalty) in zip(scores, segments):
        w = jnp.exp2((s - jnp.where(penalty > 0, BIG, top)) * SCALE2)
        t = jnp.sum(w, axis=0, keepdims=True)
        o = jnp.dot(values, w.astype(BF16), preferred_element_type=F32)
        total = t if total is None else total + t
        out = o if out is None else out + o
    live = total > 0
    inv = 1.0 / jnp.where(live, total, 1.0)
    lse = jnp.where(live, top * SCALE2 + jnp.log2(jnp.where(live, total, 1.0)), -BIG)
    return out * inv, lse


def kernel(
    chips, tokens, q_ref, kv_ref, suf_ref, new_ref, mask_ref, slot_ref, live_ref, out_ref,
    qb, kvs, sufs, news, fresh, bias, vt, svt, part_o, part_l, rs_in, rs_out, rl_in, rl_out, fin, land,
    loc_sem, sib_send, sib_recv, g_send, g_recv, o_send, o_recv, l_send, l_recv, f_send, f_recv,
):
    half = chips // 2
    node = lax.axis_index("node")
    core, chip = lax.rem(node, 2), lax.div(node, 2)
    odd, pair_no = lax.rem(chip, 2), lax.div(chip, 2)
    pos = (1 - odd) * pair_no + odd * (chips - 1 - pair_no)

    def chip_at(position):
        back = lax.div(position, half)
        return (1 - back) * 2 * position + back * (2 * (chips - 1 - position) + 1)

    def at(position):
        return {"node": chip_at(position) * 2 + core}

    sibling = {"node": node + 1 - 2 * core}
    ahead = (at(lax.rem(pos + 1, chips)), at(lax.rem(pos + chips - 1, chips)))
    pages = tokens // BT

    def behind(d, k):
        return lax.rem(pos + chips - k, chips) if d == 0 else lax.rem(pos + k, chips)

    mine = pl.multiple_of(core * HALF * DH, HALF * DH)
    theirs = pl.multiple_of((1 - core) * HALF * DH, HALF * DH)
    slot_rows = pl.ds(pl.multiple_of(core * ROWS, ROWS), ROWS)

    def views(columns, heads):
        return (
            (q_ref.at[pl.ds(heads, HALF)], qb.at[pos, :, slot_rows, :]),
            (kv_ref.at[:, :, pl.ds(columns, HALF * DH)], kvs.at[:, core]),
            (suf_ref.at[:, :, pl.ds(columns, HALF * DH)], sufs.at[:, core]),
            (fresh.at[:, :, pl.ds(columns, HALF * DH)], news.at[:, core]),
        )

    local = [
        pltpu.make_async_copy(src, dst, loc_sem.at[i])
        for i, (src, dst) in enumerate(views(mine, core * HALF))
    ]
    across = [
        pltpu.make_async_remote_copy(
            src_ref=src, dst_ref=dst, send_sem=sib_send.at[i], recv_sem=sib_recv.at[i],
            device_id=sibling,
        )
        for i, (src, dst) in enumerate(views(theirs, (1 - core) * HALF))
    ]

    def hop(d, h, piece):
        ref = qb.at[behind(d, h - 1), pl.ds(2 * piece, 2)]
        return pltpu.make_async_remote_copy(
            src_ref=ref, dst_ref=ref, send_sem=g_send.at[d, h, piece],
            recv_sem=g_recv.at[d, h, piece], device_id=ahead[d],
        )

    def landed(d, h, piece):
        ref = qb.at[behind(d, h), pl.ds(2 * piece, 2)]
        return pltpu.make_async_remote_copy(
            src_ref=ref, dst_ref=ref, send_sem=g_send.at[d, h, piece],
            recv_sem=g_recv.at[d, h, piece], device_id=ahead[d],
        )

    def stage(d, j, piece):
        heads = pl.ds(2 * piece, 2)
        return (
            pltpu.make_async_remote_copy(
                src_ref=rs_out.at[d, j, heads], dst_ref=rs_in.at[d, j, heads],
                send_sem=o_send.at[d, j, piece], recv_sem=o_recv.at[d, j, piece],
                device_id=ahead[d],
            ),
            pltpu.make_async_remote_copy(
                src_ref=rl_out.at[d, j, piece], dst_ref=rl_in.at[d, j, piece],
                send_sem=l_send.at[d, j, piece], recv_sem=l_recv.at[d, j, piece],
                device_id=ahead[d],
            ),
        )

    across.append(
        pltpu.make_async_remote_copy(
            src_ref=bias.at[core], dst_ref=bias.at[core], send_sem=sib_send.at[4],
            recv_sem=sib_recv.at[4], device_id=sibling,
        )
    )
    for copy in local[:3]:
        copy.start()
    barrier = pltpu.get_barrier_semaphore()
    for other in (sibling, *ahead):
        pl.semaphore_signal(barrier, inc=1, device_id=other)
    place16 = lax.broadcasted_iota(jnp.int32, (16, STEPS), 0)
    pick = (place16 == lax.broadcasted_iota(jnp.int32, (16, STEPS), 1)).astype(BF16)
    for i in range(2):
        fresh[i] = jnp.dot(pick, new_ref[i], preferred_element_type=F32).astype(BF16)
    requests, slots = mask_ref.shape[1], slot_ref.shape[1]
    held = lax.broadcasted_iota(jnp.int32, (requests, slots), 0) == slot_ref[...]
    visible = jnp.dot(
        mask_ref[...].astype(F32), held.astype(F32), preferred_element_type=F32
    )

    @pl.loop(0, chips)
    def _(b):
        slot = lax.broadcasted_iota(jnp.int32, (slots, LANES), 0)
        side = lax.div(lax.broadcasted_iota(jnp.int32, (slots, LANES), 1), ROWS)
        spread = (slot == 2 * chip_at(b) + side).astype(F32)
        seen = jnp.dot(visible, spread, preferred_element_type=F32)
        bias[core, b] = jnp.where(seen > 0.5, 0.0, BIG)

    page_row = lax.broadcasted_iota(jnp.int32, (pages, LANES), 0)
    page_side = lax.div(lax.broadcasted_iota(jnp.int32, (pages, LANES), 1), ROWS)
    bias[core, chips] = jnp.where((page_row < live_ref[0]) & (page_side == core), 0.0, BIG)
    local[3].start()
    pl.semaphore_wait(barrier, 3)
    for copy in across:
        copy.start()
    local[0].wait()
    across[0].wait_recv()
    for piece in range(2):
        for d in range(2):
            hop(d, 1, piece).start()

    def pass_on(h):
        for piece in range(2):
            for d in range(2):
                landed(d, h, piece).wait_recv()

                @pl.when((h + 1 < half) | (d == piece))
                def _():
                    hop(d, h + 1, piece).start()

    pass_on(1)
    for copy in local[1:]:
        copy.wait()
    for copy in across[1:]:
        copy.wait_recv()

    def columns_of(k):
        return pl.ds(pl.multiple_of(k * DH, DH), DH)

    @pl.loop(0, HALF)
    def _(k):
        for s in range(2):
            vt[k, s] = kvs[1, s, :, columns_of(k)].T
            svt[k, s] = sufs[1, s, :, columns_of(k)].T

    def shared_segments(k, blocks):
        found = []
        for s in range(2):
            for page in range(pages):
                rows = slice(page * BT, (page + 1) * BT)
                penalty = jnp.concatenate([bias[s, b, page : page + 1, :] for b in blocks], axis=1)
                found.append((kvs[0, s, rows, columns_of(k)], vt[k, s, :, rows], penalty))
        return found

    def keep(block, k, o, lse):
        part_o[block, k] = o
        part_l[block, k] = lse

    def own_block():
        token = lax.broadcasted_iota(jnp.int32, (16, LANES), 0)
        lane = lax.broadcasted_iota(jnp.int32, (16, LANES), 1)
        step = lax.rem(lax.div(lane, G), STEPS)

        @pl.loop(0, HALF)
        def _(k):
            found = shared_segments(k, [pos])
            for s in range(2):
                for page in range(sufs.shape[2] // BT):
                    rows = slice(page * BT, (page + 1) * BT)
                    penalty = bias[s, chips, page : page + 1, :]
                    found.append((sufs[0, s, rows, columns_of(k)], svt[k, s, :, rows], penalty))
                seen = (token <= step) & (lax.div(lane, ROWS) == s)
                found.append(
                    (
                        news[0, s, :, columns_of(k)],
                        news[1, s, :, columns_of(k)].T,
                        jnp.where(seen, 0.0, BIG),
                    )
                )
            keep(pos, k, *attend(qb[pos, k], found))

    def one_block(block):
        @pl.loop(0, HALF)
        def _(k):
            keep(block, k, *attend(qb[block, k], shared_segments(k, [block])))

    def two_blocks(a, b):
        @pl.loop(0, HALF)
        def _(k):
            q = jnp.concatenate([qb[a, k], qb[b, k]], axis=0)
            o, lse = attend(q, shared_segments(k, [a, b]))
            keep(a, k, o[:, :LANES], lse[:, :LANES])
            keep(b, k, o[:, LANES:], lse[:, LANES:])

    @pl.loop(2, half + 1)
    def _(h):
        @pl.when(h < half)
        def _():
            pass_on(h)

        @pl.when(h == half)
        def _():
            for d in range(2):
                landed(d, half, d).wait_recv()
            far = behind(0, half)
            one_block(far)
            for d in range(2):
                for i in range(2):
                    k = 2 * d + i
                    rs_out[d, 1, k] = part_o[far, k].astype(BF16)
                    rl_out[d, 1, d, i : i + 1, :] = part_l[far, k]
                for copy in stage(d, 1, d):
                    copy.start()

        two_blocks(behind(0, h - 1), behind(1, h - 1))

    def incoming(d, j, piece):
        for copy in stage(d, j, piece):
            copy.wait_recv()

    def received(d, j, k):
        return rs_in[d, j, k].astype(F32), rl_in[d, j, k // 2, k % 2 : k % 2 + 1, :]

    @pl.loop(2, half + 1)
    def _(j):
        for piece in range(2):
            for d in range(2):
                target = behind(1 - d, half + 1 - j)

                def add():
                    incoming(d, j - 1, piece)
                    for k in (2 * piece, 2 * piece + 1):
                        o, lse = merge(*received(d, j - 1, k), part_o[target, k], part_l[target, k])
                        rs_out[d, j, k] = o.astype(BF16)
                        rl_out[d, j, piece, k % 2 : k % 2 + 1, :] = lse

                def begin():
                    for k in (2 * piece, 2 * piece + 1):
                        rs_out[d, j, k] = part_o[target, k].astype(BF16)
                        rl_out[d, j, piece, k % 2 : k % 2 + 1, :] = part_l[target, k]

                if d == piece:
                    add()
                else:
                    pl.when(j > 2)(add)
                    pl.when(j == 2)(begin)
                for copy in stage(d, j, piece):
                    copy.start()

        pl.when(j == 2)(own_block)

    for piece in range(2):
        for d in range(2):
            incoming(d, half, piece)
        for k in (2 * piece, 2 * piece + 1):
            o, lse = merge(*received(0, half, k), part_o[pos, k], part_l[pos, k])
            o, _ = merge(o, lse, *received(1, half, k))
            fin[k] = o.T.astype(BF16)
    sib_rows = pl.ds(pl.multiple_of((1 - core) * ROWS, ROWS), ROWS)
    give = pltpu.make_async_remote_copy(
        src_ref=fin.at[:, sib_rows, :], dst_ref=land, send_sem=f_send, recv_sem=f_recv,
        device_id=sibling,
    )
    give.start()
    out_ref[pl.ds(core * HALF, HALF)] = fin[:, slot_rows, :]
    give.wait_recv()
    out_ref[pl.ds((1 - core) * HALF, HALF)] = land[...]
    give.wait_send()
    for copy in across:
        copy.wait_send()

    @pl.loop(1, half + 1)
    def _(h):
        for piece in range(2):
            for d in range(2):
                @pl.when((h < half) | (d == piece))
                def _():
                    hop(d, h, piece).wait_send()

                @pl.when((h > 1) | (d == piece))
                def _():
                    for copy in stage(d, h, piece):
                        copy.wait_send()


def per_device(queries, shared_kv, page_mask, slot_request, suffix_blocks, suffix_kv, new_kv):
    nodes = lax.axis_size("node")
    chips = nodes // 2
    half = chips // 2
    tokens = shared_kv.shape[1]
    suffix_tokens = suffix_kv.shape[2]
    pages = page_mask.shape[0]

    q = queries.reshape(STEPS, KVH, G, DH).transpose(1, 0, 2, 3).reshape(KVH, ROWS, DH)
    dma = pltpu.SemaphoreType.DMA
    grid_sems = dma((2, half + 1, 2))
    out = pl.pallas_call(
        functools.partial(kernel, chips, tokens),
        out_shape=jax.ShapeDtypeStruct((KVH, ROWS, DH), BF16),
        in_specs=[pl.BlockSpec(memory_space=pl.ANY)] * 3
        + [pl.BlockSpec(memory_space=pltpu.VMEM)] * 3
        + [pl.BlockSpec(memory_space=pltpu.SMEM)],
        out_specs=pl.BlockSpec(memory_space=pltpu.VMEM),
        scratch_shapes=[
            pltpu.VMEM((chips, HALF, LANES, DH), BF16),
            pltpu.VMEM((2, 2, tokens, HALF * DH), BF16),
            pltpu.VMEM((2, 2, suffix_tokens, HALF * DH), BF16),
            pltpu.VMEM((2, 2, 16, HALF * DH), BF16),
            pltpu.VMEM((2, 16, KVH * DH), BF16),
            pltpu.VMEM((2, chips + 1, pages, LANES), F32),
            pltpu.VMEM((HALF, 2, DH, tokens), BF16),
            pltpu.VMEM((HALF, 2, DH, suffix_tokens), BF16),
            pltpu.VMEM((chips, HALF, DH, LANES), F32),
            pltpu.VMEM((chips, HALF, 1, LANES), F32),
            pltpu.VMEM((2, half + 1, HALF, DH, LANES), BF16),
            pltpu.VMEM((2, half + 1, HALF, DH, LANES), BF16),
            pltpu.VMEM((2, half + 1, 2, 8, LANES), F32),
            pltpu.VMEM((2, half + 1, 2, 8, LANES), F32),
            pltpu.VMEM((HALF, LANES, DH), BF16),
            pltpu.VMEM((HALF, ROWS, DH), BF16),
            dma((4,)), dma((5,)), dma((5,)),
            grid_sems, grid_sems, grid_sems, grid_sems, grid_sems, grid_sems,
            dma, dma,
        ],
        compiler_params=pltpu.CompilerParams(
            collective_id=0, has_side_effects=True, vmem_limit_bytes=56 * 1024 * 1024
        ),
    )(q, shared_kv, suffix_kv[0], new_kv[0], page_mask, slot_request[None, :], suffix_blocks)
    out = out.reshape(KVH, STEPS, G, DH).transpose(1, 0, 2, 3)
    return out.reshape(1, STEPS, H * DH)


def solution(mesh):
    placed = (
        P(("grp", "node"), None, None),
        P(None, ("grp", "node"), None),
        P(("grp", "node"), None),
        P("grp"),
        P(("grp", "node")),
        P(("grp", "node"), None, None, None),
        P(("grp", "node"), None, None, None),
    )
    return jax.shard_map(
        per_device,
        mesh=mesh,
        in_specs=placed,
        out_specs=P(("grp", "node"), None, None),
        check_vma=False,
    )
```

```python
import functools

import jax
import jax.numpy as jnp
import numpy as np
from jax import lax
from jax.experimental import pallas as pl
from jax.experimental.pallas import tpu as pltpu
from jax.sharding import PartitionSpec as P

H = 128
KVH = 8
DH = 128
BT = 128
STEPS = 4
G = H // KVH
HALF = KVH // 2
ROWS = STEPS * G
LANES = 2 * ROWS
SCALE2 = float(DH ** (-0.5) * np.log2(np.e))
BIG = 1e30
F32 = jnp.float32
BF16 = jnp.bfloat16
NT = (((1,), (1,)), ((), ()))


def merge(o1, l1, o2, l2):
    top = jnp.maximum(l1, l2)
    a, b = jnp.exp2(l1 - top), jnp.exp2(l2 - top)
    both = a + b
    inv = 1.0 / both
    return o1 * (a * inv) + o2 * (b * inv), top + jnp.log2(both)


def attend(q, segments):
    scores, top = [], None
    for keys, _, penalty in segments:
        s = lax.dot_general(keys, q, NT, preferred_element_type=F32)
        scores.append(s)
        if penalty.shape[0] == 1:
            m = jnp.max(s, axis=0, keepdims=True) - penalty
        else:
            m = jnp.max(s - penalty, axis=0, keepdims=True)
        top = m if top is None else jnp.maximum(top, m)
    out, total = None, None
    for s, (_, values, penalty) in zip(scores, segments):
        w = jnp.exp2((s - jnp.where(penalty > 0, BIG, top)) * SCALE2)
        t = jnp.sum(w, axis=0, keepdims=True)
        o = jnp.dot(values, w.astype(BF16), preferred_element_type=F32)
        total = t if total is None else total + t
        out = o if out is None else out + o
    live = total > 0
    inv = 1.0 / jnp.where(live, total, 1.0)
    lse = jnp.where(live, top * SCALE2 + jnp.log2(jnp.where(live, total, 1.0)), -BIG)
    return out * inv, lse


def kernel(
    chips, tokens, q_ref, kv_ref, suf_ref, new_ref, mask_ref, slot_ref, live_ref, out_ref,
    qb, kvs, sufs, news, fresh, bias, vt, svt, part_o, part_l, rs_in, rs_out, rl_in, rl_out, fin, land,
    loc_sem, sib_send, sib_recv, g_send, g_recv, o_send, o_recv, l_send, l_recv, f_send, f_recv,
):
    half = chips // 2
    node = lax.axis_index("node")
    core, chip = lax.rem(node, 2), lax.div(node, 2)
    odd, pair_no = lax.rem(chip, 2), lax.div(chip, 2)
    pos = (1 - odd) * pair_no + odd * (chips - 1 - pair_no)

    def chip_at(position):
        back = lax.div(position, half)
        return (1 - back) * 2 * position + back * (2 * (chips - 1 - position) + 1)

    def at(position):
        return {"node": chip_at(position) * 2 + core}

    sibling = {"node": node + 1 - 2 * core}
    ahead = (at(lax.rem(pos + 1, chips)), at(lax.rem(pos + chips - 1, chips)))
    pages = tokens // BT

    def behind(d, k):
        return lax.rem(pos + chips - k, chips) if d == 0 else lax.rem(pos + k, chips)

    mine = pl.multiple_of(core * HALF * DH, HALF * DH)
    theirs = pl.multiple_of((1 - core) * HALF * DH, HALF * DH)
    slot_rows = pl.ds(pl.multiple_of(core * ROWS, ROWS), ROWS)

    def views(columns, heads):
        return (
            (q_ref.at[pl.ds(heads, HALF)], qb.at[pos, :, slot_rows, :]),
            (kv_ref.at[:, :, pl.ds(columns, HALF * DH)], kvs.at[:, core]),
            (suf_ref.at[:, :, pl.ds(columns, HALF * DH)], sufs.at[:, core]),
            (fresh.at[:, :, pl.ds(columns, HALF * DH)], news.at[:, core]),
        )

    local = [
        pltpu.make_async_copy(src, dst, loc_sem.at[i])
        for i, (src, dst) in enumerate(views(mine, core * HALF))
    ]
    across = [
        pltpu.make_async_remote_copy(
            src_ref=src, dst_ref=dst, send_sem=sib_send.at[i], recv_sem=sib_recv.at[i],
            device_id=sibling,
        )
        for i, (src, dst) in enumerate(views(theirs, (1 - core) * HALF))
    ]

    def hop(d, h, piece):
        ref = qb.at[behind(d, h - 1), pl.ds(2 * piece, 2)]
        return pltpu.make_async_remote_copy(
            src_ref=ref, dst_ref=ref, send_sem=g_send.at[d, h, piece],
            recv_sem=g_recv.at[d, h, piece], device_id=ahead[d],
        )

    def landed(d, h, piece):
        ref = qb.at[behind(d, h), pl.ds(2 * piece, 2)]
        return pltpu.make_async_remote_copy(
            src_ref=ref, dst_ref=ref, send_sem=g_send.at[d, h, piece],
            recv_sem=g_recv.at[d, h, piece], device_id=ahead[d],
        )

    def stage(d, j, piece):
        heads = pl.ds(2 * piece, 2)
        return (
            pltpu.make_async_remote_copy(
                src_ref=rs_out.at[d, j, heads], dst_ref=rs_in.at[d, j, heads],
                send_sem=o_send.at[d, j, piece], recv_sem=o_recv.at[d, j, piece],
                device_id=ahead[d],
            ),
            pltpu.make_async_remote_copy(
                src_ref=rl_out.at[d, j, piece], dst_ref=rl_in.at[d, j, piece],
                send_sem=l_send.at[d, j, piece], recv_sem=l_recv.at[d, j, piece],
                device_id=ahead[d],
            ),
        )

    across.append(
        pltpu.make_async_remote_copy(
            src_ref=bias.at[core], dst_ref=bias.at[core], send_sem=sib_send.at[4],
            recv_sem=sib_recv.at[4], device_id=sibling,
        )
    )
    for copy in local[:3]:
        copy.start()
    barrier = pltpu.get_barrier_semaphore()
    for other in (sibling, *ahead):
        pl.semaphore_signal(barrier, inc=1, device_id=other)
    pl.semaphore_wait(barrier, 3)
    for copy in across[:3]:
        copy.start()
    local[0].wait()
    across[0].wait_recv()
    for piece in range(2):
        for d in range(2):
            hop(d, 1, piece).start()

    place16 = lax.broadcasted_iota(jnp.int32, (16, STEPS), 0)
    pick = (place16 == lax.broadcasted_iota(jnp.int32, (16, STEPS), 1)).astype(BF16)
    for i in range(2):
        fresh[i] = jnp.dot(pick, new_ref[i], preferred_element_type=F32).astype(BF16)
    requests, slots = mask_ref.shape[1], slot_ref.shape[1]
    held = lax.broadcasted_iota(jnp.int32, (requests, slots), 0) == slot_ref[...]
    visible = jnp.dot(
        mask_ref[...].astype(F32), held.astype(F32), preferred_element_type=F32
    )

    @pl.loop(0, chips)
    def _(b):
        slot = lax.broadcasted_iota(jnp.int32, (slots, LANES), 0)
        side = lax.div(lax.broadcasted_iota(jnp.int32, (slots, LANES), 1), ROWS)
        spread = (slot == 2 * chip_at(b) + side).astype(F32)
        seen = jnp.dot(visible, spread, preferred_element_type=F32)
        bias[core, b] = jnp.where(seen > 0.5, 0.0, BIG)

    page_row = lax.broadcasted_iota(jnp.int32, (pages, LANES), 0)
    page_side = lax.div(lax.broadcasted_iota(jnp.int32, (pages, LANES), 1), ROWS)
    bias[core, chips] = jnp.where((page_row < live_ref[0]) & (page_side == core), 0.0, BIG)
    local[3].start()
    for copy in across[3:]:
        copy.start()
    def pass_on(h):
        for piece in range(2):
            for d in range(2):
                landed(d, h, piece).wait_recv()

                @pl.when((h + 1 < half) | (d == piece))
                def _():
                    hop(d, h + 1, piece).start()

    pass_on(1)
    for copy in local[1:]:
        copy.wait()
    for copy in across[1:]:
        copy.wait_recv()

    def columns_of(k):
        return pl.ds(pl.multiple_of(k * DH, DH), DH)

    @pl.loop(0, HALF)
    def _(k):
        for s in range(2):
            vt[k, s] = kvs[1, s, :, columns_of(k)].T
            svt[k, s] = sufs[1, s, :, columns_of(k)].T

    def shared_segments(k, blocks):
        found = []
        for s in range(2):
            for page in range(pages):
                rows = slice(page * BT, (page + 1) * BT)
                penalty = jnp.concatenate([bias[s, b, page : page + 1, :] for b in blocks], axis=1)
                found.append((kvs[0, s, rows, columns_of(k)], vt[k, s, :, rows], penalty))
        return found

    def keep(block, k, o, lse):
        part_o[block, k] = o
        part_l[block, k] = lse

    def own_block():
        token = lax.broadcasted_iota(jnp.int32, (16, LANES), 0)
        lane = lax.broadcasted_iota(jnp.int32, (16, LANES), 1)
        step = lax.rem(lane, STEPS)

        @pl.loop(0, HALF, unroll=4)
        def _(k):
            found = shared_segments(k, [pos])
            for s in range(2):
                for page in range(sufs.shape[2] // BT):
                    rows = slice(page * BT, (page + 1) * BT)
                    penalty = bias[s, chips, page : page + 1, :]
                    found.append((sufs[0, s, rows, columns_of(k)], svt[k, s, :, rows], penalty))
                seen = (token <= step) & (lax.div(lane, ROWS) == s)
                found.append(
                    (
                        news[0, s, :, columns_of(k)],
                        news[1, s, :, columns_of(k)].T,
                        jnp.where(seen, 0.0, BIG),
                    )
                )
            keep(pos, k, *attend(qb[pos, k], found))

    def one_block(block):
        @pl.loop(0, HALF, unroll=4)
        def _(k):
            keep(block, k, *attend(qb[block, k], shared_segments(k, [block])))

    def two_blocks(a, b):
        @pl.loop(0, HALF, unroll=4)
        def _(k):
            q = jnp.concatenate([qb[a, k], qb[b, k]], axis=0)
            o, lse = attend(q, shared_segments(k, [a, b]))
            keep(a, k, o[:, :LANES], lse[:, :LANES])
            keep(b, k, o[:, LANES:], lse[:, LANES:])

    @pl.loop(2, half + 1)
    def _(h):
        @pl.when(h < half)
        def _():
            pass_on(h)

        @pl.when(h == half)
        def _():
            for d in range(2):
                landed(d, half, d).wait_recv()
            far = behind(0, half)
            for d in range(2):
                for i in range(2):
                    k = 2 * d + i
                    o, lse = attend(qb[far, k], shared_segments(k, [far]))
                    rs_out[d, 1, k] = o.astype(BF16)
                    rl_out[d, 1, d, i : i + 1, :] = lse
                for copy in stage(d, 1, d):
                    copy.start()

        two_blocks(behind(0, h - 1), behind(1, h - 1))

    def incoming(d, j, piece):
        for copy in stage(d, j, piece):
            copy.wait_recv()

    def received(d, j, k):
        return rs_in[d, j, k].astype(F32), rl_in[d, j, k // 2, k % 2 : k % 2 + 1, :]

    @pl.loop(2, half + 1)
    def _(j):
        for piece in range(2):
            for d in range(2):
                target = behind(1 - d, half + 1 - j)

                def add():
                    incoming(d, j - 1, piece)
                    for k in (2 * piece, 2 * piece + 1):
                        o, lse = merge(*received(d, j - 1, k), part_o[target, k], part_l[target, k])
                        rs_out[d, j, k] = o.astype(BF16)
                        rl_out[d, j, piece, k % 2 : k % 2 + 1, :] = lse

                def begin():
                    for k in (2 * piece, 2 * piece + 1):
                        rs_out[d, j, k] = part_o[target, k].astype(BF16)
                        rl_out[d, j, piece, k % 2 : k % 2 + 1, :] = part_l[target, k]

                if d == piece:
                    add()
                else:
                    pl.when(j > 2)(add)
                    pl.when(j == 2)(begin)
                for copy in stage(d, j, piece):
                    copy.start()

        pl.when(j == 2)(own_block)

    for piece in range(2):
        for d in range(2):
            incoming(d, half, piece)
        for k in (2 * piece, 2 * piece + 1):
            o, lse = merge(*received(0, half, k), part_o[pos, k], part_l[pos, k])
            o, _ = merge(o, lse, *received(1, half, k))
            fin[k] = o.T.astype(BF16)
    sib_rows = pl.ds(pl.multiple_of((1 - core) * ROWS, ROWS), ROWS)
    give = pltpu.make_async_remote_copy(
        src_ref=fin.at[:, sib_rows, :], dst_ref=land, send_sem=f_send, recv_sem=f_recv,
        device_id=sibling,
    )
    give.start()
    out_ref[pl.ds(core * HALF, HALF)] = fin[:, slot_rows, :]
    give.wait_recv()
    out_ref[pl.ds((1 - core) * HALF, HALF)] = land[...]
    give.wait_send()
    for copy in across:
        copy.wait_send()

    @pl.loop(1, half + 1)
    def _(h):
        for piece in range(2):
            for d in range(2):
                @pl.when((h < half) | (d == piece))
                def _():
                    hop(d, h, piece).wait_send()

                @pl.when((h > 1) | (d == piece))
                def _():
                    for copy in stage(d, h, piece):
                        copy.wait_send()


def per_device(queries, shared_kv, page_mask, slot_request, suffix_blocks, suffix_kv, new_kv):
    nodes = lax.axis_size("node")
    chips = nodes // 2
    half = chips // 2
    tokens = shared_kv.shape[1]
    suffix_tokens = suffix_kv.shape[2]
    pages = page_mask.shape[0]

    q = queries.reshape(STEPS, H, DH).transpose(1, 0, 2).reshape(KVH, ROWS, DH)
    dma = pltpu.SemaphoreType.DMA
    grid_sems = dma((2, half + 1, 2))
    out = pl.pallas_call(
        functools.partial(kernel, chips, tokens),
        out_shape=jax.ShapeDtypeStruct((KVH, ROWS, DH), BF16),
        in_specs=[pl.BlockSpec(memory_space=pl.ANY)] * 3
        + [pl.BlockSpec(memory_space=pltpu.VMEM)] * 3
        + [pl.BlockSpec(memory_space=pltpu.SMEM)],
        out_specs=pl.BlockSpec(memory_space=pltpu.VMEM),
        scratch_shapes=[
            pltpu.VMEM((chips, HALF, LANES, DH), BF16),
            pltpu.VMEM((2, 2, tokens, HALF * DH), BF16),
            pltpu.VMEM((2, 2, suffix_tokens, HALF * DH), BF16),
            pltpu.VMEM((2, 2, 16, HALF * DH), BF16),
            pltpu.VMEM((2, 16, KVH * DH), BF16),
            pltpu.VMEM((2, chips + 1, pages, LANES), F32),
            pltpu.VMEM((HALF, 2, DH, tokens), BF16),
            pltpu.VMEM((HALF, 2, DH, suffix_tokens), BF16),
            pltpu.VMEM((chips, HALF, DH, LANES), F32),
            pltpu.VMEM((chips, HALF, 1, LANES), F32),
            pltpu.VMEM((2, half + 1, HALF, DH, LANES), BF16),
            pltpu.VMEM((2, half + 1, HALF, DH, LANES), BF16),
            pltpu.VMEM((2, half + 1, 2, 8, LANES), F32),
            pltpu.VMEM((2, half + 1, 2, 8, LANES), F32),
            pltpu.VMEM((HALF, LANES, DH), BF16),
            pltpu.VMEM((HALF, ROWS, DH), BF16),
            dma((4,)), dma((5,)), dma((5,)),
            grid_sems, grid_sems, grid_sems, grid_sems, grid_sems, grid_sems,
            dma, dma,
        ],
        compiler_params=pltpu.CompilerParams(
            collective_id=0, has_side_effects=True, vmem_limit_bytes=56 * 1024 * 1024
        ),
    )(q, shared_kv, suffix_kv[0], new_kv[0], page_mask, slot_request[None, :], suffix_blocks)
    out = out.reshape(H, STEPS, DH).transpose(1, 0, 2)
    return out.reshape(1, STEPS, H * DH)


def solution(mesh):
    placed = (
        P(("grp", "node"), None, None),
        P(None, ("grp", "node"), None),
        P(("grp", "node"), None),
        P("grp"),
        P(("grp", "node")),
        P(("grp", "node"), None, None, None),
        P(("grp", "node"), None, None, None),
    )
    return jax.shard_map(
        per_device,
        mesh=mesh,
        in_specs=placed,
        out_specs=P(("grp", "node"), None, None),
        check_vma=False,
    )
```

```python
import functools

import jax
import jax.numpy as jnp
import numpy as np
from jax import lax
from jax.experimental import pallas as pl
from jax.experimental.pallas import tpu as pltpu
from jax.sharding import PartitionSpec as P

H = 128
KVH = 8
DH = 128
BT = 128
STEPS = 4
G = H // KVH
HALF = KVH // 2
ROWS = STEPS * G
LANES = 2 * ROWS
SCALE2 = float(DH ** (-0.5) * np.log2(np.e))
BIG = 1e30
F32 = jnp.float32
BF16 = jnp.bfloat16
NT = (((1,), (1,)), ((), ()))


def merge(o1, l1, o2, l2):
    top = jnp.maximum(l1, l2)
    a, b = jnp.exp2(l1 - top), jnp.exp2(l2 - top)
    both = a + b
    inv = 1.0 / both
    return o1 * (a * inv) + o2 * (b * inv), top + jnp.log2(both)


def attend(q, segments):
    scores, top = [], None
    for keys, _, penalty in segments:
        s = lax.dot_general(keys, q, NT, preferred_element_type=F32)
        scores.append(s)
        if penalty.shape[0] == 1:
            m = jnp.max(s, axis=0, keepdims=True) - penalty
        else:
            m = jnp.max(s - penalty, axis=0, keepdims=True)
        top = m if top is None else jnp.maximum(top, m)
    out, total = None, None
    for s, (_, values, penalty) in zip(scores, segments):
        w = jnp.exp2((s - jnp.where(penalty > 0, BIG, top)) * SCALE2)
        t = jnp.sum(w, axis=0, keepdims=True)
        o = jnp.dot(values, w.astype(BF16), preferred_element_type=F32)
        total = t if total is None else total + t
        out = o if out is None else out + o
    live = total > 0
    inv = 1.0 / jnp.where(live, total, 1.0)
    lse = jnp.where(live, top * SCALE2 + jnp.log2(jnp.where(live, total, 1.0)), -BIG)
    return out * inv, lse


def kernel(
    chips, tokens, q_ref, kv_ref, suf_ref, new_ref, mask_ref, slot_ref, live_ref, out_ref,
    qb, kvs, sufs, news, fresh, bias, vt, svt, part_o, part_l, rs_in, rs_out, rl_in, rl_out, fin, land,
    loc_sem, sib_send, sib_recv, g_send, g_recv, o_send, o_recv, l_send, l_recv, f_send, f_recv,
):
    half = chips // 2
    node = lax.axis_index("node")
    core, chip = lax.rem(node, 2), lax.div(node, 2)
    odd, pair_no = lax.rem(chip, 2), lax.div(chip, 2)
    pos = (1 - odd) * pair_no + odd * (chips - 1 - pair_no)

    def chip_at(position):
        back = lax.div(position, half)
        return (1 - back) * 2 * position + back * (2 * (chips - 1 - position) + 1)

    def at(position):
        return {"node": chip_at(position) * 2 + core}

    sibling = {"node": node + 1 - 2 * core}
    ahead = (at(lax.rem(pos + 1, chips)), at(lax.rem(pos + chips - 1, chips)))
    pages = tokens // BT

    def behind(d, k):
        return lax.rem(pos + chips - k, chips) if d == 0 else lax.rem(pos + k, chips)

    mine = pl.multiple_of(core * HALF * DH, HALF * DH)
    theirs = pl.multiple_of((1 - core) * HALF * DH, HALF * DH)
    slot_rows = pl.ds(pl.multiple_of(core * ROWS, ROWS), ROWS)

    def views(columns, heads):
        return (
            (q_ref.at[pl.ds(heads, HALF)], qb.at[pos, :, slot_rows, :]),
            (kv_ref.at[:, :, pl.ds(columns, HALF * DH)], kvs.at[:, core]),
            (suf_ref.at[:, :, pl.ds(columns, HALF * DH)], sufs.at[:, core]),
            (fresh.at[:, :, pl.ds(columns, HALF * DH)], news.at[:, core]),
        )

    local = [
        pltpu.make_async_copy(src, dst, loc_sem.at[i])
        for i, (src, dst) in enumerate(views(mine, core * HALF))
    ]
    across = [
        pltpu.make_async_remote_copy(
            src_ref=src, dst_ref=dst, send_sem=sib_send.at[i], recv_sem=sib_recv.at[i],
            device_id=sibling,
        )
        for i, (src, dst) in enumerate(views(theirs, (1 - core) * HALF))
    ]

    def hop(d, h, piece):
        ref = qb.at[behind(d, h - 1), pl.ds(2 * piece, 2)]
        return pltpu.make_async_remote_copy(
            src_ref=ref, dst_ref=ref, send_sem=g_send.at[d, h, piece],
            recv_sem=g_recv.at[d, h, piece], device_id=ahead[d],
        )

    def landed(d, h, piece):
        ref = qb.at[behind(d, h), pl.ds(2 * piece, 2)]
        return pltpu.make_async_remote_copy(
            src_ref=ref, dst_ref=ref, send_sem=g_send.at[d, h, piece],
            recv_sem=g_recv.at[d, h, piece], device_id=ahead[d],
        )

    def stage(d, j, piece):
        heads = pl.ds(2 * piece, 2)
        return (
            pltpu.make_async_remote_copy(
                src_ref=rs_out.at[d, j, heads], dst_ref=rs_in.at[d, j, heads],
                send_sem=o_send.at[d, j, piece], recv_sem=o_recv.at[d, j, piece],
                device_id=ahead[d],
            ),
            pltpu.make_async_remote_copy(
                src_ref=rl_out.at[d, j, piece], dst_ref=rl_in.at[d, j, piece],
                send_sem=l_send.at[d, j, piece], recv_sem=l_recv.at[d, j, piece],
                device_id=ahead[d],
            ),
        )

    across.append(
        pltpu.make_async_remote_copy(
            src_ref=bias.at[core], dst_ref=bias.at[core], send_sem=sib_send.at[4],
            recv_sem=sib_recv.at[4], device_id=sibling,
        )
    )
    for copy in local[:3]:
        copy.start()
    barrier = pltpu.get_barrier_semaphore()
    for other in (sibling, *ahead):
        pl.semaphore_signal(barrier, inc=1, device_id=other)
    pl.semaphore_wait(barrier, 3)
    for copy in across[:3]:
        copy.start()
    local[0].wait()
    across[0].wait_recv()
    for piece in range(2):
        for d in range(2):
            hop(d, 1, piece).start()

    place16 = lax.broadcasted_iota(jnp.int32, (16, STEPS), 0)
    pick = (place16 == lax.broadcasted_iota(jnp.int32, (16, STEPS), 1)).astype(BF16)
    for i in range(2):
        fresh[i] = jnp.dot(pick, new_ref[i], preferred_element_type=F32).astype(BF16)
    requests, slots = mask_ref.shape[1], slot_ref.shape[1]
    held = lax.broadcasted_iota(jnp.int32, (requests, slots), 0) == slot_ref[...]
    visible = jnp.dot(
        mask_ref[...].astype(F32), held.astype(F32), preferred_element_type=F32
    )

    @pl.loop(0, chips)
    def _(b):
        slot = lax.broadcasted_iota(jnp.int32, (slots, LANES), 0)
        side = lax.div(lax.broadcasted_iota(jnp.int32, (slots, LANES), 1), ROWS)
        spread = (slot == 2 * chip_at(b) + side).astype(F32)
        seen = jnp.dot(visible, spread, preferred_element_type=F32)
        bias[core, b] = jnp.where(seen > 0.5, 0.0, BIG)

    page_row = lax.broadcasted_iota(jnp.int32, (pages, LANES), 0)
    page_side = lax.div(lax.broadcasted_iota(jnp.int32, (pages, LANES), 1), ROWS)
    bias[core, chips] = jnp.where((page_row < live_ref[0]) & (page_side == core), 0.0, BIG)
    local[3].start()
    for copy in across[3:]:
        copy.start()
    def pass_on(h):
        for piece in range(2):
            for d in range(2):
                landed(d, h, piece).wait_recv()

                @pl.when((h + 1 < half) | (d == piece))
                def _():
                    hop(d, h + 1, piece).start()

    pass_on(1)
    for copy in local[1:]:
        copy.wait()
    for copy in across[1:]:
        copy.wait_recv()

    def columns_of(k):
        return pl.ds(pl.multiple_of(k * DH, DH), DH)

    @pl.loop(0, HALF)
    def _(k):
        for s in range(2):
            vt[k, s] = kvs[1, s, :, columns_of(k)].T
            svt[k, s] = sufs[1, s, :, columns_of(k)].T

    def shared_segments(k, blocks):
        found = []
        for s in range(2):
            for page in range(pages):
                rows = slice(page * BT, (page + 1) * BT)
                penalty = jnp.concatenate([bias[s, b, page : page + 1, :] for b in blocks], axis=1)
                found.append((kvs[0, s, rows, columns_of(k)], vt[k, s, :, rows], penalty))
        return found

    def keep(block, k, o, lse):
        part_o[block, k] = o
        part_l[block, k] = lse

    def own_block():
        token = lax.broadcasted_iota(jnp.int32, (16, LANES), 0)
        lane = lax.broadcasted_iota(jnp.int32, (16, LANES), 1)
        step = lax.rem(lane, STEPS)

        @pl.loop(0, HALF, unroll=4)
        def _(k):
            found = shared_segments(k, [pos])
            for s in range(2):
                for page in range(sufs.shape[2] // BT):
                    rows = slice(page * BT, (page + 1) * BT)
                    penalty = bias[s, chips, page : page + 1, :]
                    found.append((sufs[0, s, rows, columns_of(k)], svt[k, s, :, rows], penalty))
                seen = (token <= step) & (lax.div(lane, ROWS) == s)
                found.append(
                    (
                        news[0, s, :, columns_of(k)],
                        news[1, s, :, columns_of(k)].T,
                        jnp.where(seen, 0.0, BIG),
                    )
                )
            keep(pos, k, *attend(qb[pos, k], found))

    def one_block(block):
        @pl.loop(0, HALF, unroll=4)
        def _(k):
            keep(block, k, *attend(qb[block, k], shared_segments(k, [block])))

    def two_blocks(a, b):
        @pl.loop(0, HALF, unroll=4)
        def _(k):
            q = jnp.concatenate([qb[a, k], qb[b, k]], axis=0)
            o, lse = attend(q, shared_segments(k, [a, b]))
            keep(a, k, o[:, :LANES], lse[:, :LANES])
            keep(b, k, o[:, LANES:], lse[:, LANES:])

    @pl.loop(2, half + 1)
    def _(h):
        @pl.when(h < half)
        def _():
            pass_on(h)

        @pl.when(h == half)
        def _():
            for d in range(2):
                landed(d, half, d).wait_recv()
            far = behind(0, half)
            for d in range(2):
                for i in range(2):
                    k = 2 * d + i
                    o, lse = attend(qb[far, k], shared_segments(k, [far]))
                    rs_out[d, 1, k] = o.astype(BF16)
                    rl_out[d, 1, d, i : i + 1, :] = lse
                for copy in stage(d, 1, d):
                    copy.start()

        @pl.when(h != half - 1)
        def _():
            two_blocks(behind(0, h - 1), behind(1, h - 1))

        pl.when(h == half - 1)(own_block)

    def incoming(d, j, piece):
        for copy in stage(d, j, piece):
            copy.wait_recv()

    def received(d, j, k):
        return rs_in[d, j, k].astype(F32), rl_in[d, j, k // 2, k % 2 : k % 2 + 1, :]

    @pl.loop(2, half + 1)
    def _(j):
        for piece in range(2):
            for d in range(2):
                target = behind(1 - d, half + 1 - j)

                def add():
                    incoming(d, j - 1, piece)
                    for k in (2 * piece, 2 * piece + 1):
                        o, lse = merge(*received(d, j - 1, k), part_o[target, k], part_l[target, k])
                        rs_out[d, j, k] = o.astype(BF16)
                        rl_out[d, j, piece, k % 2 : k % 2 + 1, :] = lse

                def begin():
                    for k in (2 * piece, 2 * piece + 1):
                        rs_out[d, j, k] = part_o[target, k].astype(BF16)
                        rl_out[d, j, piece, k % 2 : k % 2 + 1, :] = part_l[target, k]

                if d == piece:
                    add()
                else:
                    pl.when(j > 2)(add)
                    pl.when(j == 2)(begin)
                for copy in stage(d, j, piece):
                    copy.start()

        @pl.when(j == 2)
        def _():
            two_blocks(behind(0, half - 2), behind(1, half - 2))

    for piece in range(2):
        for d in range(2):
            incoming(d, half, piece)
        for k in (2 * piece, 2 * piece + 1):
            o, lse = merge(*received(0, half, k), part_o[pos, k], part_l[pos, k])
            o, _ = merge(o, lse, *received(1, half, k))
            fin[k] = o.T.astype(BF16)
    sib_rows = pl.ds(pl.multiple_of((1 - core) * ROWS, ROWS), ROWS)
    give = pltpu.make_async_remote_copy(
        src_ref=fin.at[:, sib_rows, :], dst_ref=land, send_sem=f_send, recv_sem=f_recv,
        device_id=sibling,
    )
    give.start()
    out_ref[pl.ds(core * HALF, HALF)] = fin[:, slot_rows, :]
    give.wait_recv()
    out_ref[pl.ds((1 - core) * HALF, HALF)] = land[...]
    give.wait_send()
    for copy in across:
        copy.wait_send()

    @pl.loop(1, half + 1)
    def _(h):
        for piece in range(2):
            for d in range(2):
                @pl.when((h < half) | (d == piece))
                def _():
                    hop(d, h, piece).wait_send()

                @pl.when((h > 1) | (d == piece))
                def _():
                    for copy in stage(d, h, piece):
                        copy.wait_send()


def per_device(queries, shared_kv, page_mask, slot_request, suffix_blocks, suffix_kv, new_kv):
    nodes = lax.axis_size("node")
    chips = nodes // 2
    half = chips // 2
    tokens = shared_kv.shape[1]
    suffix_tokens = suffix_kv.shape[2]
    pages = page_mask.shape[0]

    q = queries.reshape(STEPS, H, DH).transpose(1, 0, 2).reshape(KVH, ROWS, DH)
    dma = pltpu.SemaphoreType.DMA
    grid_sems = dma((2, half + 1, 2))
    out = pl.pallas_call(
        functools.partial(kernel, chips, tokens),
        out_shape=jax.ShapeDtypeStruct((KVH, ROWS, DH), BF16),
        in_specs=[pl.BlockSpec(memory_space=pl.ANY)] * 3
        + [pl.BlockSpec(memory_space=pltpu.VMEM)] * 3
        + [pl.BlockSpec(memory_space=pltpu.SMEM)],
        out_specs=pl.BlockSpec(memory_space=pltpu.VMEM),
        scratch_shapes=[
            pltpu.VMEM((chips, HALF, LANES, DH), BF16),
            pltpu.VMEM((2, 2, tokens, HALF * DH), BF16),
            pltpu.VMEM((2, 2, suffix_tokens, HALF * DH), BF16),
            pltpu.VMEM((2, 2, 16, HALF * DH), BF16),
            pltpu.VMEM((2, 16, KVH * DH), BF16),
            pltpu.VMEM((2, chips + 1, pages, LANES), F32),
            pltpu.VMEM((HALF, 2, DH, tokens), BF16),
            pltpu.VMEM((HALF, 2, DH, suffix_tokens), BF16),
            pltpu.VMEM((chips, HALF, DH, LANES), F32),
            pltpu.VMEM((chips, HALF, 1, LANES), F32),
            pltpu.VMEM((2, half + 1, HALF, DH, LANES), BF16),
            pltpu.VMEM((2, half + 1, HALF, DH, LANES), BF16),
            pltpu.VMEM((2, half + 1, 2, 8, LANES), F32),
            pltpu.VMEM((2, half + 1, 2, 8, LANES), F32),
            pltpu.VMEM((HALF, LANES, DH), BF16),
            pltpu.VMEM((HALF, ROWS, DH), BF16),
            dma((4,)), dma((5,)), dma((5,)),
            grid_sems, grid_sems, grid_sems, grid_sems, grid_sems, grid_sems,
            dma, dma,
        ],
        compiler_params=pltpu.CompilerParams(
            collective_id=0, has_side_effects=True, vmem_limit_bytes=56 * 1024 * 1024
        ),
    )(q, shared_kv, suffix_kv[0], new_kv[0], page_mask, slot_request[None, :], suffix_blocks)
    out = out.reshape(H, STEPS, DH).transpose(1, 0, 2)
    return out.reshape(1, STEPS, H * DH)


def solution(mesh):
    placed = (
        P(("grp", "node"), None, None),
        P(None, ("grp", "node"), None),
        P(("grp", "node"), None),
        P("grp"),
        P(("grp", "node")),
        P(("grp", "node"), None, None, None),
        P(("grp", "node"), None, None, None),
    )
    return jax.shard_map(
        per_device,
        mesh=mesh,
        in_specs=placed,
        out_specs=P(("grp", "node"), None, None),
        check_vma=False,
    )
```
